32 devices in a mesh: rep: 8 (over z, core), shard: 4 (over y, x).
Axes of the slice: x: 2, y: 2, z: 4, core: 2. Of those that a mesh axis runs over, the one named last changes fastest.
Arguments:
- hidden_in: bfloat16 [12288, 2048], P(('rep', 'shard')), may hold values from -6 to 6
- segment_ids: int32 [12288], P(('rep', 'shard')), may hold values from 0 to 3, as said below
- attn_norm: bfloat16 [2048], P('shard'), may hold values from 0.5 to 1.5
- attn_router: bfloat16 [2048, 2], P('shard'), may hold values from -0.09375 to 0.09375
- kv_weight: bfloat16 [2048, 4096], P('shard'), may hold values from -0.125 to 0.125
- query_weight: bfloat16 [2, 2048, 2048], P(None, 'shard'), may hold values from -0.125 to 0.125
- out_weight: bfloat16 [2, 2048, 2048], P(None, 'shard'), may hold values from -1 to 1
- mlp_norm: bfloat16 [2048], P('shard'), may hold values from 0.5 to 1.5
- mlp_router: bfloat16 [2048, 2], P('shard'), may hold values from -0.09375 to 0.09375
- gate_weight: bfloat16 [2, 2048, 5632], P(None, None, 'shard'), may hold values from -0.125 to 0.125
- up_weight: bfloat16 [2, 2048, 5632], P(None, None, 'shard'), may hold values from -0.125 to 0.125
- down_weight: bfloat16 [2, 5632, 2048], P(None, 'shard'), may hold values from -0.078125 to 0.078125
- cotangent: bfloat16 [12288, 2048], P(('rep', 'shard')), may hold values from -6 to 6
Outputs:
- output: bfloat16 [12288, 2048], P(('rep', 'shard'))
- input_grad: float32 [12288, 2048], P(('rep', 'shard'))
- attn_norm_grad: float32 [2048], P('shard')
- attn_router_grad: float32 [2048, 2], P('shard')
- kv_weight_grad: float32 [2048, 4096], P('shard')
- query_weight_grad: float32 [2, 2048, 2048], P(None, 'shard')
- out_weight_grad: float32 [2, 2048, 2048], P(None, 'shard')
- mlp_norm_grad: float32 [2048], P('shard')
- mlp_router_grad: float32 [2048, 2], P('shard')
- gate_weight_grad: float32 [2, 2048, 5632], P(None, None, ('shard', 'rep'))
- up_weight_grad: float32 [2, 2048, 5632], P(None, None, ('shard', 'rep'))
- down_weight_grad: float32 [2, 5632, 2048], P(None, ('shard', 'rep'))
The draws below stay inside these ranges and needn't reach their ends.
Inputs may be any that keep to these rules, and one draw needn't show every extreme that they name: `segment_ids`: within each sequence of 1536 rows the segment numbers never fall and begin at 0.
All inputs are finite; a program needn't handle non-finite values.
Results may differ from the reference program's by a relative error of at most 0.02.
Values may be sent and summed in bfloat16 or wider, within the bound.
No kernel may reach another device: no remote copies, remote signals or barrier semaphores. Data moves between devices by JAX's collectives and lax.ppermute only.
A program may use at most 576 MiB of HBM per device.

```python
import jax
import jax.numpy as jnp
from jax import lax

D = 2048
HEADS = 16
HEAD = 128
FF = 5632
ATT_EXP = 2
MLP_EXP = 2
WIN = 1024
SEQ_LEN = 1536
TOK_DEV = 384
TOKENS = 12288


def draw_segment_ids(key, part):
    key = jax.random.fold_in(key, 7)
    seq_count = TOKENS // SEQ_LEN
    first_key, second_key, third_key = jax.random.split(key, 3)
    start_cut = jax.random.randint(first_key, (seq_count, 1), 2, TOK_DEV)
    early_cut = jax.random.randint(second_key, (seq_count, 1), 1, start_cut)
    late_cut = jax.random.randint(third_key, (seq_count, 1), SEQ_LEN - TOK_DEV + 1, SEQ_LEN)
    positions = jnp.arange(SEQ_LEN, dtype=jnp.int32)[None, :]
    numbers = (positions >= early_cut).astype(jnp.int32) + (positions >= start_cut).astype(jnp.int32) + (positions >= late_cut).astype(jnp.int32)
    return numbers.reshape(TOKENS)


def levels(key, shape, cuts, smallest, high):
    level, own = 1.0, jax.random.fold_in(key, 6)
    for dim, blocks in cuts:
        heights = jnp.exp(jax.random.uniform(jax.random.fold_in(own, dim), (blocks,), jnp.float32, smallest / len(cuts), high / len(cuts)))
        level = level * jnp.repeat(heights, shape[dim] // blocks).reshape([-1 if axis == dim else 1 for axis in range(len(shape))])
    return level


def gaussian(stream_key, extent, deviation, bound, shards=(), held_as=jnp.bfloat16):
    drawn = deviation * jax.random.normal(stream_key, extent, jnp.float32)
    if shards:
        drawn = drawn * levels(stream_key, extent, shards, -0.22, 0.18)
    return jnp.clip(drawn, -bound, bound).astype(held_as)


def setup_inputs(seed: int = 0) -> dict:
    arg_keys = jax.random.split(jax.random.key(seed), 14)
    hidden_in = gaussian(arg_keys[0], (TOKENS, D), 1.0, 6.0, ((0, 32),))
    segment_ids = draw_segment_ids(jax.random.fold_in(arg_keys[13], 71), 0)
    attn_norm = jnp.clip(1.0 + 0.1 * jax.random.normal(arg_keys[2], (D,), jnp.float32), 0.5, 1.5).astype(jnp.bfloat16)
    attn_router = gaussian(arg_keys[3], (D, ATT_EXP), (D * 16 // 9) ** -0.5, 0.09375, ((0, 4),))
    kv_weight = gaussian(arg_keys[4], (D, 2 * HEADS * HEAD), D ** -0.5, 0.125, ((0, 4),))
    query_weight = gaussian(arg_keys[5], (ATT_EXP, D, HEADS * HEAD), D ** -0.5, 0.125, ((1, 4),))
    out_weight = gaussian(arg_keys[6], (ATT_EXP, HEADS * HEAD, D), (max(HEADS * HEAD // 64, 1)) ** -0.5, 1.0, ((1, 4),))
    mlp_norm = jnp.clip(1.0 + 0.1 * jax.random.normal(arg_keys[7], (D,), jnp.float32), 0.5, 1.5).astype(jnp.bfloat16)
    mlp_router = gaussian(arg_keys[8], (D, MLP_EXP), (D * 16 // 9) ** -0.5, 0.09375, ((0, 4),))
    gate_weight = gaussian(arg_keys[9], (MLP_EXP, D, FF), D ** -0.5, 0.125, ((2, 4),))
    up_weight = gaussian(arg_keys[10], (MLP_EXP, D, FF), D ** -0.5, 0.125, ((2, 4),))
    down_weight = gaussian(arg_keys[11], (MLP_EXP, FF, D), FF ** -0.5, 0.078125, ((1, 4),))
    cotangent = gaussian(arg_keys[12], (TOKENS, D), 1.0, 6.0, ((0, 32),))
    return dict(hidden_in=hidden_in, segment_ids=segment_ids, attn_norm=attn_norm, attn_router=attn_router, kv_weight=kv_weight, query_weight=query_weight, out_weight=out_weight, mlp_norm=mlp_norm, mlp_router=mlp_router, gate_weight=gate_weight, up_weight=up_weight, down_weight=down_weight, cotangent=cotangent)


EPSILON = 1e-06
THETA = 10000.0
HIGHEST = lax.Precision.HIGHEST

@jax.custom_vjp
def low(v):
    return lax.optimization_barrier(v.astype(jnp.bfloat16)).astype(jnp.float32)

@jax.custom_vjp
def low_back(v):
    return v

def low_keep(v):
    return (low(v), None)

def low_pass(kept, grad):
    return (grad,)

def back_keep(v):
    return (v, None)

def back_low(kept, grad):
    return (low(grad),)
low.defvjp(low_keep, low_pass)
low_back.defvjp(back_keep, back_low)

def rotate(field, position):
    half_width = field.shape[-1] // 2
    frequency = THETA ** (-jnp.arange(half_width, dtype=jnp.float32) / half_width)
    angle = position.astype(jnp.float32)[:, None] * frequency[None, :]
    cos_table = jnp.cos(angle)[:, None, :]
    sin_table = jnp.sin(angle)[:, None, :]
    first_half = field[..., :half_width]
    second_half = field[..., half_width:]
    return jnp.concatenate([first_half * cos_table - second_half * sin_table, second_half * cos_table + first_half * sin_table], -1)

def layer_forward(hidden, segments, attn_norm, attn_router, kv_weight, query_weight, out_weight, mlp_norm, mlp_router, gate_weight, up_weight, down_weight):
    length = hidden.shape[0]
    position = jnp.arange(length, dtype=jnp.int32)
    scale_one = lax.rsqrt(lax.optimization_barrier(jnp.mean(hidden * hidden, -1, keepdims=True)) + EPSILON)
    normed = low(hidden * scale_one * attn_norm)
    gate_one = jax.nn.softmax(jnp.dot(normed, attn_router, precision=HIGHEST), -1)
    keyval = low_back(jnp.dot(normed, kv_weight, precision=HIGHEST))
    kv_width = keyval.shape[1] // 2
    head_count = kv_width // HEAD
    all_keys = low(rotate(keyval[:, :kv_width].reshape(length, head_count, HEAD), position))
    all_values = low(keyval[:, kv_width:].reshape(length, head_count, HEAD))
    expert_count = query_weight.shape[0]
    queries = low_back(jnp.einsum('td,edf->etf', normed, query_weight, precision=HIGHEST))
    queries = low(rotate(queries.reshape(expert_count, length, head_count, HEAD), position))
    row_block = min(512, length)

    def attend(start):
        query_rows = lax.dynamic_slice_in_dim(queries, start, row_block, 1)
        raw = jnp.einsum('ebhd,khd->ehbk', query_rows, all_keys, precision=HIGHEST)
        scores = low_back(raw * HEAD ** (-0.5))
        query_place = start + jnp.arange(row_block, dtype=jnp.int32)
        query_segment = lax.dynamic_slice_in_dim(segments, start, row_block)
        distance = query_place[:, None] - position[None, :]
        allowed = (query_segment[:, None] == segments[None, :]) & (distance >= 0) & (distance < WIN)
        scores = jnp.where(allowed, scores, -1e+30)
        row_top = lax.optimization_barrier(jnp.max(scores, -1, keepdims=True))
        weights = jnp.exp(scores - row_top)
        prob_low = low(weights / lax.optimization_barrier(jnp.sum(weights, -1, keepdims=True)))
        return jnp.einsum('ehbk,khd->ebhd', prob_low, all_values, precision=HIGHEST)
    starts = jnp.arange(length // row_block, dtype=jnp.int32) * row_block
    heads_out = lax.map(jax.checkpoint(attend), starts)
    heads_out = heads_out.transpose(1, 0, 2, 3, 4).reshape(expert_count, length, kv_width)
    heads_out = low(low_back(heads_out))
    branch = low_back(jnp.einsum('etf,efd->etd', heads_out, out_weight, precision=HIGHEST))
    middle = hidden + lax.optimization_barrier(jnp.sum(gate_one.T[:, :, None] * branch, 0))
    scale_two = lax.rsqrt(lax.optimization_barrier(jnp.mean(middle * middle, -1, keepdims=True)) + EPSILON)
    normed_two = low(middle * scale_two * mlp_norm)
    gate_two = jax.nn.softmax(jnp.dot(normed_two, mlp_router, precision=HIGHEST), -1)
    gate_pre = low_back(jnp.einsum('td,edf->etf', normed_two, gate_weight, precision=HIGHEST))
    up_pre = low_back(jnp.einsum('td,edf->etf', normed_two, up_weight, precision=HIGHEST))
    inner_act = low(jax.nn.silu(gate_pre) * up_pre)
    expert_out = low_back(jnp.einsum('etf,efd->etd', inner_act, down_weight, precision=HIGHEST))
    return middle + lax.optimization_barrier(jnp.sum(gate_two.T[:, :, None] * expert_out, 0))

def reference(hidden_in, segment_ids, attn_norm, attn_router, kv_weight, query_weight, out_weight, mlp_norm, mlp_router, gate_weight, up_weight, down_weight, cotangent):
    params = tuple((array_item.astype(jnp.float32) for array_item in (attn_norm, attn_router, kv_weight, query_weight, out_weight, mlp_norm, mlp_router, gate_weight, up_weight, down_weight)))
    seq_count = hidden_in.shape[0] // SEQ_LEN
    model_width = hidden_in.shape[1]
    hidden_rows = hidden_in.astype(jnp.float32).reshape(seq_count, SEQ_LEN, model_width)
    segment_rows = segment_ids.reshape(seq_count, SEQ_LEN)
    cot_rows = cotangent.astype(jnp.float32).reshape(seq_count, SEQ_LEN, model_width)

    def one_sequence(totals, inputs):
        hidden_seq, segments, cot_seq = inputs

        def forward(hidden_arg, *weight_args):
            return layer_forward(hidden_arg, segments, *weight_args)
        result, pullback = jax.vjp(forward, hidden_seq, *params)
        grads = pullback(cot_seq)
        totals = tuple((running + increment for running, increment in zip(totals, grads[1:])))
        return (totals, (result, grads[0]))
    zero_grads = tuple((jnp.zeros_like(array_item) for array_item in params))
    totals, (results, input_grads) = lax.scan(one_sequence, zero_grads, (hidden_rows, segment_rows, cot_rows))
    return (results.reshape(-1, model_width).astype(jnp.bfloat16), input_grads.reshape(-1, model_width), totals[0], totals[1], totals[2], totals[3], totals[4], totals[5], totals[6], totals[7], totals[8], totals[9])
```

```python
import jax
import jax.numpy as jnp
from jax import lax
from jax.experimental import pallas as pl
from jax.experimental.pallas import tpu as pltpu
from jax.sharding import Mesh, PartitionSpec as P

HEAD = 128
WIN = 1024
EPSILON = 1e-06
THETA = 10000.0
HIGHEST = lax.Precision.HIGHEST
BF16 = jnp.bfloat16
F32 = jnp.float32
LOG2E = 1.4426950408889634
MIB = 1 << 20
QUERY_ROWS = 256


def swap(value, axis, bits):
    count = lax.axis_size(axis)
    return lax.ppermute(value, axis, [(i, i ^ bits) for i in range(count)])


def together(*values):
    return lax.optimization_barrier(values)


def bit_orders(count):
    bits = [1 << b for b in range(count.bit_length() - 1)]
    return [bits[i:] + bits[:i] for i in range(len(bits))] or [[]]


def ways(held, axis):
    orders = bit_orders(lax.axis_size(axis))
    return [(orders[i % len(orders)], part) for i, part in enumerate(held)]


def gather_start(block, axis="shard"):
    orders = bit_orders(lax.axis_size(axis))
    return [{0: part} for part in together(*jnp.split(block, len(orders), 0))]


def gather_step(held, step, axis="shard"):
    after = []
    for order, have in ways(held, axis):
        bit = order[step]
        after.append({**have, **{r ^ bit: swap(v, axis, bit) for r, v in have.items()}})
    return after


def gather_end(held):
    return [jnp.concatenate([have[r] for have in held], 0) for r in range(len(held[0]))]


def gather_blocks(block, axis="shard"):
    held = gather_start(block, axis)
    for step in range(len(bit_orders(lax.axis_size(axis))[0])):
        held = gather_step(held, step, axis)
    return gather_end(held)


def scatter_start(blocks, axis="shard"):
    orders = bit_orders(lax.axis_size(axis))
    held = [dict() for _ in orders]
    for r, block in enumerate(blocks):
        for have, part in zip(held, jnp.split(block, len(orders), 0)):
            have[r] = part
    return held


def scatter_cut(held, step, axis="shard"):
    cut = []
    for order, have in ways(held, axis):
        bit = order[-1 - step]
        kept = {r: v for r, v in have.items() if not r & bit}
        cut.append((kept, jnp.concatenate([have[r ^ bit].astype(BF16) for r in kept], 0)))
    sent = together(*[sent for _, sent in cut])
    return [(kept, new) for (kept, _), new in zip(cut, sent)]


def scatter_send(cut, step, axis="shard"):
    pairs = []
    for order, (kept, sent) in ways(cut, axis):
        pairs.append((kept, swap(sent, axis, order[-1 - step])))
    return pairs


def arrived(pairs, *beside):
    got, *beside = together([got for _, got in pairs], *beside)
    return [(kept, new) for (kept, _), new in zip(pairs, got)], *beside


def scatter_step(held, step, axis="shard"):
    return scatter_send(scatter_cut(held, step, axis), step, axis)


def scatter_add(pairs):
    held = []
    for kept, got in pairs:
        got = jnp.split(got, len(kept), 0)
        held.append({r: kept[r].astype(F32) + new.astype(F32) for r, new in zip(kept, got)})
    return held


def scatter_end(held):
    return jnp.concatenate([have[0] for have in held], 0)


def scatter_sum(blocks, beside=(), axis="shard"):
    held = scatter_start(blocks, axis)
    beside = list(beside)
    for step in range(len(bit_orders(lax.axis_size(axis))[0])):
        pairs = scatter_step(held, step, axis)
        if step < len(beside):
            pairs, beside[step] = arrived(pairs, beside[step])
        held = scatter_add(pairs)
    return scatter_end(held), beside


def scatter_small(blocks, axis="shard"):
    total = blocks[0]
    for r in range(1, lax.axis_size(axis)):
        total = total + swap(blocks[r], axis, r)
    return total


REPLICAS = ("chip", "core")


def replica_scatter(whole):
    return lax.psum_scatter(whole, REPLICAS, scatter_dimension=1, tiled=True)


def chip_sum(whole, axis):
    core = lax.axis_index("core")
    kept = lax.dynamic_index_in_dim(whole, core, axis, keepdims=False)
    sent = lax.dynamic_index_in_dim(whole, 1 - core, axis, keepdims=False)
    return kept, swap(sent, "core", 1)


def add_low(kept, got):
    return (kept.astype(F32) + got.astype(F32)).astype(BF16)


def pick(options, index):
    chosen = options[0]
    for i, option in enumerate(options[1:], 1):
        chosen = jnp.where(index == i, option, chosen)
    return chosen


def in_order(blocks, me, base=None):
    rows = blocks[0].shape[0]
    whole = base
    if base is None:
        whole = jnp.zeros((rows * len(blocks),) + blocks[0].shape[1:], blocks[0].dtype)
    for r, block in enumerate(blocks):
        start = ((me ^ r) * rows,) + (0,) * (block.ndim - 1)
        whole = lax.dynamic_update_slice(whole, block, start)
    return whole


def by_distance(whole, me, count):
    rows = whole.shape[0] // count
    return [lax.dynamic_slice_in_dim(whole, (me ^ r) * rows, rows, 0) for r in range(count)]


def rotation_tables(length):
    half = HEAD // 2
    frequency = THETA ** (-jnp.arange(half, dtype=F32) / half)
    angle = jnp.arange(length, dtype=F32)[:, None] * frequency[None, :]
    cos, sin = jnp.cos(angle), jnp.sin(angle)
    return jnp.concatenate([cos, cos], 1), jnp.concatenate([-sin, sin], 1)


def turn(head, cos, sin):
    return head * cos + pltpu.roll(head, HEAD // 2, 1) * sin


def nt(a, b):
    return lax.dot_general(a, b, (((1,), (1,)), ((), ())), preferred_element_type=F32)


def nn(a, b):
    return lax.dot_general(a, b, (((1,), (0,)), ((), ())), preferred_element_type=F32)


def tn(a, b):
    return lax.dot_general(a, b, (((0,), (0,)), ((), ())), preferred_element_type=F32)


def project_kernel(normed, weight, cos, sin, out):
    kind = pl.program_id(1)
    product = nn(normed[...], weight[0])

    @pl.when(kind == 1)
    def _():
        out[0] = product.astype(BF16)

    @pl.when(kind != 1)
    def _():
        for start in range(0, product.shape[1], HEAD):
            head = product[:, start : start + HEAD]
            out[0, :, start : start + HEAD] = turn(head, cos[...], sin[...]).astype(BF16)


def project(normed, weight, cos, sin):
    seq, width = normed.shape
    kinds, _, cols = weight.shape
    rows = seq
    once = dict(pipeline_mode=pl.Buffered(1))
    return pl.pallas_call(
        project_kernel,
        grid=(seq // rows, kinds),
        in_specs=[
            pl.BlockSpec((rows, width), lambda i, k: (i, 0), **once),
            pl.BlockSpec((1, width, cols), lambda i, k: (k, 0, 0)),
            pl.BlockSpec((rows, HEAD), lambda i, k: (i, 0), **once),
            pl.BlockSpec((rows, HEAD), lambda i, k: (i, 0), **once),
        ],
        out_specs=pl.BlockSpec((1, rows, cols), lambda i, k: (k, i, 0)),
        out_shape=jax.ShapeDtypeStruct((kinds, seq, cols), BF16),
        compiler_params=pltpu.CompilerParams(vmem_limit_bytes=48 * MIB),
        cost_estimate=pl.CostEstimate(
            flops=2 * seq * width * kinds * cols,
            bytes_accessed=2 * (seq * width + kinds * cols * (width + seq)),
            transcendentals=0,
        ),
    )(normed, weight, cos, sin)


def key_span(block):
    low = max(0, block * QUERY_ROWS - WIN + 1) // QUERY_ROWS * QUERY_ROWS
    return low, (block + 1) * QUERY_ROWS


def forbid(query_segment, key_segment, query_place, key_place):
    distance = query_place - key_place
    allowed = (query_segment == key_segment) & (distance >= 0) & (distance < WIN)
    return jnp.where(allowed, 0.0, -1e30).astype(F32)


def attend_kernel(experts, blocks, seg_col, seg_row, keys, values, *rest):
    queries, (out, stats, bias) = rest[:experts], rest[experts:]
    block, head = pl.program_id(0), pl.program_id(1)
    factor = HEAD ** (-0.5) * LOG2E
    rows = experts * QUERY_ROWS

    def step(at):
        low, high = key_span(at)
        span = high - low

        @pl.when(head == 0)
        def _():
            shape = (QUERY_ROWS, span)
            bias[:, :span] = forbid(
                seg_col[...],
                seg_row[:, low:high],
                at * QUERY_ROWS + lax.broadcasted_iota(jnp.int32, shape, 0),
                low + lax.broadcasted_iota(jnp.int32, shape, 1),
            )

        query = jnp.concatenate([q[0] for q in queries], 0)
        scores = nt(query, keys[0, low:high])
        scores = scores + jnp.concatenate([bias[:, :span]] * experts, 0)
        top = jnp.max(scores, -1, keepdims=True)
        weights = jnp.exp2((scores - top) * factor)
        total = jnp.sum(weights, -1, keepdims=True)
        mixed = nn(weights.astype(BF16), values[0, low:high]) / total
        level = jnp.broadcast_to(top * factor + jnp.log2(total), (rows, HEAD)).T
        for expert in range(experts):
            part = slice(expert * QUERY_ROWS, (expert + 1) * QUERY_ROWS)
            out[expert] = mixed[part].astype(BF16)
            stats[0, expert : expert + 1, :] = level[0:1, part]

    for at in range(blocks):
        pl.when(block == at)(lambda at=at: step(at))


def attend(projected, segments):
    kinds, seq, cols = projected.shape
    experts, heads, blocks = kinds - 2, cols // HEAD, seq // QUERY_ROWS
    widest = max(high - low for low, high in map(key_span, range(blocks)))
    pairs = sum(high - low for low, high in map(key_span, range(blocks))) * QUERY_ROWS
    query_specs = [
        pl.BlockSpec((1, QUERY_ROWS, HEAD), lambda i, h, e=e: (2 + e, i, h)) for e in range(experts)
    ]
    return pl.pallas_call(
        lambda *refs: attend_kernel(experts, blocks, *refs),
        grid=(blocks, heads),
        in_specs=[
            pl.BlockSpec((QUERY_ROWS, 1), lambda i, h: (i, 0)),
            pl.BlockSpec((1, seq), lambda i, h: (0, 0)),
            pl.BlockSpec((1, seq, HEAD), lambda i, h: (0, 0, h)),
            pl.BlockSpec((1, seq, HEAD), lambda i, h: (1, 0, h)),
        ]
        + query_specs,
        out_specs=[
            pl.BlockSpec((experts, QUERY_ROWS, HEAD), lambda i, h: (0, i, h)),
            pl.BlockSpec((1, experts, QUERY_ROWS), lambda i, h: (h, 0, i)),
        ],
        out_shape=[
            jax.ShapeDtypeStruct((experts, seq, cols), BF16),
            jax.ShapeDtypeStruct((heads, experts, seq), F32),
        ],
        scratch_shapes=[pltpu.VMEM((QUERY_ROWS, widest), F32)],
        compiler_params=pltpu.CompilerParams(vmem_limit_bytes=48 * MIB),
        cost_estimate=pl.CostEstimate(
            flops=8 * pairs * experts * heads * HEAD,
            bytes_accessed=2 * seq * cols * (2 + 2 * experts),
            transcendentals=pairs * experts * heads,
        ),
    )(segments[:, None], segments[None, :], *([projected] * (2 + experts)))


def attend_back_kernel(experts, blocks, seg_row, seg_col, cos, sin, keys, values, *rest):
    queries = rest[:experts]
    d_heads, stats, delta, out, bias, d_keys, d_values = rest[experts:]
    head, block = pl.program_id(0), pl.program_id(1)
    scale = HEAD ** (-0.5)
    factor = scale * LOG2E

    @pl.when(block == 0)
    def _():
        d_keys[...] = jnp.zeros_like(d_keys)
        d_values[...] = jnp.zeros_like(d_values)

    def step(at):
        low, high = key_span(at)
        span = high - low
        own = slice(at * QUERY_ROWS, (at + 1) * QUERY_ROWS)

        @pl.when(head == 0)
        def _():
            shape = (span, QUERY_ROWS)
            bias[at, :span, :] = forbid(
                seg_row[...],
                seg_col[low:high],
                at * QUERY_ROWS + lax.broadcasted_iota(jnp.int32, shape, 1),
                low + lax.broadcasted_iota(jnp.int32, shape, 0),
            )

        for expert in range(experts):
            query = queries[expert][0]
            d_head = d_heads[expert]
            key, value = keys[0, low:high], values[0, low:high]
            scores = nt(key, query) * factor + bias[at, :span, :]
            probs = jnp.exp2(scores - stats[0, expert : expert + 1, :])
            d_probs = nt(value, d_head)
            d_scores = (probs * (d_probs - delta[0, expert : expert + 1, :])).astype(BF16)
            d_values[low:high] += nn(probs.astype(BF16), d_head)
            d_keys[low:high] += nn(d_scores, query)
            d_query = tn(d_scores, key) * scale
            out[2 + expert, own, :] = turn(d_query, cos[own], -sin[own]).astype(BF16)

    for at in range(blocks):
        pl.when(block == at)(lambda at=at: step(at))

    @pl.when(block == blocks - 1)
    def _():
        out[0] = turn(d_keys[...] * scale, cos[...], -sin[...]).astype(BF16)
        out[1] = d_values[...].astype(BF16)


def attend_back(projected, segments, cos, sin, d_heads, stats, delta):
    kinds, seq, cols = projected.shape
    experts, heads, blocks = kinds - 2, cols // HEAD, seq // QUERY_ROWS
    widest = max(high - low for low, high in map(key_span, range(blocks)))
    pairs = sum(high - low for low, high in map(key_span, range(blocks))) * QUERY_ROWS
    query_specs = [
        pl.BlockSpec((1, QUERY_ROWS, HEAD), lambda h, i, e=e: (2 + e, i, h)) for e in range(experts)
    ]
    row_spec = pl.BlockSpec((1, experts, QUERY_ROWS), lambda h, i: (h, 0, i))
    return pl.pallas_call(
        lambda *refs: attend_back_kernel(experts, blocks, *refs),
        grid=(heads, blocks),
        in_specs=[
            pl.BlockSpec((1, QUERY_ROWS), lambda h, i: (0, i)),
            pl.BlockSpec((seq, 1), lambda h, i: (0, 0)),
            pl.BlockSpec((seq, HEAD), lambda h, i: (0, 0)),
            pl.BlockSpec((seq, HEAD), lambda h, i: (0, 0)),
            pl.BlockSpec((1, seq, HEAD), lambda h, i: (0, 0, h)),
            pl.BlockSpec((1, seq, HEAD), lambda h, i: (1, 0, h)),
        ]
        + query_specs
        + [
            pl.BlockSpec((experts, QUERY_ROWS, HEAD), lambda h, i: (0, i, h)),
            row_spec,
            row_spec,
        ],
        out_specs=pl.BlockSpec((kinds, seq, HEAD), lambda h, i: (0, 0, h)),
        out_shape=jax.ShapeDtypeStruct((kinds, seq, cols), BF16),
        scratch_shapes=[
            pltpu.VMEM((blocks, widest, QUERY_ROWS), F32),
            pltpu.VMEM((seq, HEAD), F32),
            pltpu.VMEM((seq, HEAD), F32),
        ],
        compiler_params=pltpu.CompilerParams(vmem_limit_bytes=48 * MIB),
        cost_estimate=pl.CostEstimate(
            flops=20 * pairs * experts * heads * HEAD,
            bytes_accessed=2 * seq * cols * (2 * kinds + experts),
            transcendentals=pairs * experts * heads,
        ),
    )(
        segments[None, :],
        segments[:, None],
        cos,
        sin,
        *([projected] * (2 + experts)),
        d_heads,
        stats,
        delta,
    )


def norm_back(d_normed, hidden, inv_scale, gain):
    scaled_grad = d_normed * gain
    return inv_scale * scaled_grad - hidden * inv_scale**3 * jnp.mean(
        scaled_grad * hidden, -1, keepdims=True
    )


def swiglu_kernel(expert, gate_pre, up_pre, d_act, gates, d_both, act, term):
    rows, width = gate_pre.shape
    lanes, step = 128, 32
    lanes = lanes if width % lanes == 0 else width
    step = step if rows % step == 0 else rows

    def part(i, carry):
        at = pl.ds(pl.multiple_of(i * step, step), step)
        gate = gates[at, expert : expert + 1]
        total = jnp.zeros((step, lanes), F32)
        for start in range(0, width, lanes):
            cut = slice(start, start + lanes)
            pre = gate_pre[at, cut].astype(F32)
            up = up_pre[at, cut].astype(F32)
            raw = d_act[at, cut].astype(F32)
            sigmoid = 0.5 * jnp.tanh(0.5 * pre) + 0.5
            silu = pre * sigmoid
            inner = silu * up
            total = total + inner * raw
            act[at, cut] = (inner * gate).astype(BF16)
            d_inner = raw * gate
            slope = sigmoid + silu * (1.0 - sigmoid)
            d_both[at, cut] = (d_inner * up * slope).astype(BF16)
            d_both[at, width + start : width + start + lanes] = (d_inner * silu).astype(BF16)
        term[at, :] = jnp.sum(total, -1, keepdims=True)
        return carry

    lax.fori_loop(0, rows // step, part, 0)


def swiglu(expert, gate_pre, up_pre, d_act, gates):
    seq, hidden = gate_pre.shape
    rows = 256 if seq % 256 == 0 else seq
    return pl.pallas_call(
        lambda *refs: swiglu_kernel(expert, *refs),
        grid=(seq // rows,),
        in_specs=[
            pl.BlockSpec((rows, hidden), lambda i: (i, 0)),
            pl.BlockSpec((rows, hidden), lambda i: (i, 0)),
            pl.BlockSpec((rows, hidden), lambda i: (i, 0)),
            pl.BlockSpec((rows, gates.shape[1]), lambda i: (i, 0)),
        ],
        out_specs=[
            pl.BlockSpec((rows, 2 * hidden), lambda i: (i, 0)),
            pl.BlockSpec((rows, hidden), lambda i: (i, 0)),
            pl.BlockSpec((rows, 1), lambda i: (i, 0)),
        ],
        out_shape=[
            jax.ShapeDtypeStruct((seq, 2 * hidden), BF16),
            jax.ShapeDtypeStruct((seq, hidden), BF16),
            jax.ShapeDtypeStruct((seq, 1), F32),
        ],
        compiler_params=pltpu.CompilerParams(vmem_limit_bytes=48 * MIB),
        cost_estimate=pl.CostEstimate(
            flops=20 * seq * hidden, bytes_accessed=12 * seq * hidden, transcendentals=seq * hidden
        ),
    )(gate_pre, up_pre, d_act, gates)


def heads_back_kernel(d_middle, out_weight, heads_out, gates, d_heads, terms, grads, total):
    block = pl.program_id(0)
    experts, cols, _ = out_weight.shape
    rows = d_middle.shape[0]

    @pl.when(block == 0)
    def _():
        total[...] = jnp.zeros_like(total)

    lane = lax.broadcasted_iota(jnp.int32, (rows, HEAD), 1)
    table = jnp.zeros((rows, HEAD), F32)
    count = experts * (cols // HEAD)
    for expert in range(experts):
        gate = gates[:, expert : expert + 1]
        back = nt(d_middle[...], out_weight[expert])
        heads = heads_out[expert].astype(F32)
        pairing = back * heads
        for head in range(cols // HEAD):
            term = jnp.sum(pairing[:, head * HEAD : (head + 1) * HEAD], -1, keepdims=True)
            at = head * experts + expert
            table = table + jnp.where(lane == at, term, 0.0)
            table = table + jnp.where(lane == count + at, term * gate, 0.0)
        d_heads[expert] = (back * gate).astype(BF16)
        total[expert] += tn((heads * gate).astype(BF16), d_middle[...])
    terms[...] = table.T[: 2 * count]

    @pl.when(block == pl.num_programs(0) - 1)
    def _():
        _, _, chips, blocks, piece, width = grads.shape
        for chip in range(chips):
            for core in range(2):
                at = (2 * chip + core) * piece
                for j in range(blocks):
                    cut = slice(j * width, (j + 1) * width)
                    grads[core, :, chip, j] = total[:, at : at + piece, cut].astype(BF16)


def heads_back(d_middle, out_weight, heads_out, gates, chips):
    experts, seq, cols = heads_out.shape
    depth = d_middle.shape[1]
    rows = 512 if seq % 512 == 0 else seq
    count = experts * (cols // HEAD)
    split = (2, experts, chips, depth // cols, cols // chips // 2, cols)
    return pl.pallas_call(
        heads_back_kernel,
        grid=(seq // rows,),
        in_specs=[
            pl.BlockSpec((rows, depth), lambda i: (i, 0)),
            pl.BlockSpec((experts, cols, depth), lambda i: (0, 0, 0)),
            pl.BlockSpec((experts, rows, cols), lambda i: (0, i, 0)),
            pl.BlockSpec((rows, experts), lambda i: (i, 0)),
        ],
        out_specs=[
            pl.BlockSpec((experts, rows, cols), lambda i: (0, i, 0)),
            pl.BlockSpec((2 * count, rows), lambda i: (0, i)),
            pl.BlockSpec(split, lambda i: (0,) * 6),
        ],
        out_shape=[
            jax.ShapeDtypeStruct((experts, seq, cols), BF16),
            jax.ShapeDtypeStruct((2 * count, seq), F32),
            jax.ShapeDtypeStruct(split, BF16),
        ],
        scratch_shapes=[pltpu.VMEM((experts, cols, depth), F32)],
        compiler_params=pltpu.CompilerParams(vmem_limit_bytes=56 * MIB),
        cost_estimate=pl.CostEstimate(
            flops=8 * seq * depth * cols * experts // 2,
            bytes_accessed=2 * (seq * depth + 2 * experts * cols * (seq + depth)),
            transcendentals=0,
        ),
    )(d_middle, out_weight, heads_out, gates)


def lay_out_kernel(beside, core, mine, other, *outs):
    experts, piece, width = outs[-1].shape

    def lay(source):
        for kind in range(beside):
            rows_of = source[0, kind * piece : (kind + 1) * piece]
            outs[0][:, kind * width : (kind + 1) * width] = rows_of.astype(F32)
        for expert in range(experts):
            at = (beside + expert) * piece
            outs[-1][expert] = source[0, at : at + piece].astype(F32)

    pl.when(core[0] == pl.program_id(1))(lambda: lay(mine))
    pl.when(core[0] != pl.program_id(1))(lambda: lay(other))


def lay_out(core, mine, other, experts, piece, beside):
    chips, rows, width = mine.shape
    own = 2 * chips * piece
    out_specs = [pl.BlockSpec((experts, piece, width), lambda j, k: (0, 2 * j + k, 0))]
    out_shape = [jax.ShapeDtypeStruct((experts, own, width), F32)]
    if beside:
        out_specs.insert(0, pl.BlockSpec((piece, beside * width), lambda j, k: (2 * j + k, 0)))
        out_shape.insert(0, jax.ShapeDtypeStruct((own, beside * width), F32))
    return pl.pallas_call(
        lambda *refs: lay_out_kernel(beside, *refs),
        grid=(chips, 2),
        in_specs=[
            pl.BlockSpec(memory_space=pltpu.SMEM),
            pl.BlockSpec((1, rows, width), lambda j, k: (j, 0, 0)),
            pl.BlockSpec((1, rows, width), lambda j, k: (j, 0, 0)),
        ],
        out_specs=out_specs,
        out_shape=out_shape,
        compiler_params=pltpu.CompilerParams(vmem_limit_bytes=48 * MIB),
        cost_estimate=pl.CostEstimate(
            flops=0,
            bytes_accessed=4 * chips * rows * width + 4 * own * width * (beside + experts),
            transcendentals=0,
        ),
    )(core.reshape(1).astype(jnp.int32), mine, other)


def router_back(d_gates, gates):
    return gates * (d_gates - jnp.sum(gates * d_gates, -1, keepdims=True))


def tn_product(a, b):
    return mm("td,tf->df", a, b).astype(BF16)


def by_router(d_logit, router):
    columns = [(d_logit[:, e : e + 1], router[:, e].astype(F32)) for e in range(router.shape[1])]
    return sum(d * row[None, :] for d, row in columns)


def mm(spec, a, b):
    return jnp.einsum(spec, a, b, preferred_element_type=F32)


def on_device(
    hidden_in,
    segment_ids,
    attn_norm,
    attn_router,
    kv_weight,
    query_weight,
    out_weight,
    mlp_norm,
    mlp_router,
    gate_weight,
    up_weight,
    down_weight,
    cotangent,
):
    rows, width = hidden_in.shape
    count = lax.axis_size("shard")
    me = lax.axis_index("shard")
    core = lax.axis_index("core")
    seq = rows * count
    own_d = kv_weight.shape[0]
    experts = query_weight.shape[0]
    cols = query_weight.shape[2] // count
    head_count = cols // HEAD
    mlp_experts = gate_weight.shape[0]
    score_scale = HEAD ** (-0.5)

    cos, sin = rotation_tables(seq)

    small = jnp.concatenate(
        [
            attn_norm,
            mlp_norm,
            attn_router.T.reshape(-1),
            mlp_router.T.reshape(-1),
            segment_ids.astype(BF16),
        ]
    )
    small = jnp.pad(small, (0, -small.shape[0] % (16 * cols))).reshape(-1, cols)
    small_rows = small.shape[0]
    kinds = 2 + experts
    chips, chip = lax.axis_size("chip"), lax.axis_index("chip")
    owners = 2 * chips
    replica = 2 * chip + core
    piece = own_d // owners

    def columns(owner, start, size):
        at = owner * cols
        return jnp.stack(
            [lax.dynamic_slice(kv_weight, (start, at), (size, cols))]
            + [lax.dynamic_slice(kv_weight, (start, count * cols + at), (size, cols))]
            + [lax.dynamic_slice(w, (start, at), (size, cols)) for w in query_weight]
        )

    def message(owner):
        return jnp.concatenate([columns(owner, replica * piece, piece).reshape(-1, cols), small], 0)

    fetched = [swap(message(me ^ r), "shard", r) for r in range(1, count)]
    held = gather_step(gather_start(hidden_in), 0)
    joined = [jnp.concatenate([gate_weight[0], up_weight[0]], 1)]
    fetched, held, joined = together(fetched, held, joined)
    small = [small] + [rows_of[-small_rows:] for rows_of in fetched]
    fetched = jnp.stack([rows_of[:-small_rows].reshape(kinds, piece, cols) for rows_of in fetched])
    shares = lax.all_gather(fetched, REPLICAS, axis=0)
    weight = jnp.zeros((kinds, width, cols), BF16)
    weight = lax.dynamic_update_slice(weight, columns(me, 0, own_d), (0, me * own_d, 0))
    rounds = len(bit_orders(count)[0])
    for step in range(1, rounds):
        held = gather_step(held, step)
    held, weight = together(held, weight)
    small = jnp.stack([pick(small, me ^ owner) for owner in range(count)]).reshape(count, -1)
    bounds = [0]
    for size in (own_d, own_d, own_d * experts, own_d * mlp_experts, rows):
        bounds.append(bounds[-1] + size)
    pieces = [small[:, a:b] for a, b in zip(bounds, bounds[1:])]
    norm_one = pieces[0].reshape(width).astype(F32)
    norm_two = pieces[1].reshape(width).astype(F32)
    router_one = pieces[2].reshape(count, experts, own_d).transpose(0, 2, 1).reshape(width, experts)
    router_two = (
        pieces[3].reshape(count, mlp_experts, own_d).transpose(0, 2, 1).reshape(width, mlp_experts)
    )
    segments = pieces[4].reshape(seq).astype(jnp.int32)

    hidden_low = in_order(gather_end(held), me)
    hidden = hidden_low.astype(F32)
    scale_one = lax.rsqrt(jnp.mean(hidden * hidden, -1, keepdims=True) + EPSILON)
    normed = (hidden * scale_one * norm_one).astype(BF16)
    normed, cos, sin, weight, shares = together(normed, cos, sin, weight, shares)
    for r in range(1, count):
        rows_of = shares[:, r - 1].transpose(1, 0, 2, 3).reshape(kinds, own_d, cols)
        weight = lax.dynamic_update_slice(weight, rows_of, (0, (me ^ r) * own_d, 0))
    gate_one = jax.nn.softmax(jnp.dot(normed, router_one, preferred_element_type=F32), -1)
    projected = project(normed, weight, cos, sin)

    cot_ready, _ = together(cotangent, weight)
    wide_cot = lax.all_gather(cot_ready, "shard", axis=0, tiled=True)
    heads_out, stats = attend(projected, segments)
    heads_out, wide_cot = together(heads_out, wide_cot)
    for expert in range(experts):
        weighted = gate_one[:, expert : expert + 1] * jnp.dot(
            heads_out[expert], out_weight[expert], preferred_element_type=F32
        )
        attn_mix = weighted if expert == 0 else attn_mix + weighted
    own_hidden = hidden_in.astype(F32)
    attn_mix, wide_cot = together(attn_mix.astype(BF16), wide_cot)
    d_act = [mm("td,fd->tf", wide_cot, down_weight[0]).astype(BF16)]
    joined += [jnp.concatenate(both, 1) for both in zip(gate_weight[1:], up_weight[1:])]
    attn_sum, ((wide_cot, d_act), joined) = scatter_sum(
        by_distance(attn_mix, me, count), [(wide_cot, d_act), joined]
    )
    middle = own_hidden + attn_sum
    scale_two = lax.rsqrt(jnp.mean(middle * middle, -1, keepdims=True) + EPSILON)
    normed_two = (middle * scale_two * norm_two).astype(BF16)

    for expert in range(1, mlp_experts):
        d_act.append(mm("td,fd->tf", wide_cot, down_weight[expert]).astype(BF16))
    held = gather_start(normed_two)
    for step in range(rounds):
        held = gather_step(held, step)
    held, d_act = together(held, d_act)
    wide_normed = in_order(gather_end(held), me, hidden_low)
    wide_gate = jax.nn.softmax(jnp.dot(wide_normed, router_two, preferred_element_type=F32), -1)
    d_both = []
    acts = []
    gate_terms = []
    expert_grads = []
    for expert in range(mlp_experts):
        gate_pre = mm("td,df->tf", wide_normed, gate_weight[expert]).astype(BF16)
        up_pre = mm("td,df->tf", wide_normed, up_weight[expert]).astype(BF16)
        both, act, term = swiglu(expert, gate_pre, up_pre, d_act[expert], wide_gate)
        if expert == 0:
            grads = mm("tf,td->fd", both, wide_normed).astype(BF16)
            grads, wide_normed = together(grads, wide_normed)
            expert_grads.append(replica_scatter(grads.reshape(2, -1, width)))
        d_both.append(both)
        acts.append(act)
        gate_terms.append(term)
    d_logit_two = router_back(jnp.concatenate(gate_terms, -1), wide_gate)
    wide_grad = sum(mm("tf,df->td", d, w) for d, w in zip(d_both, joined))
    wide_grad = (wide_grad + by_router(d_logit_two, router_two)).astype(BF16)
    wide_grad, d_both = together(wide_grad, d_both)
    late_grads = [mm("tf,td->fd", d, wide_normed).astype(BF16) for d in d_both[1:]]
    d_normed_two, (late_grads,) = scatter_sum(by_distance(wide_grad, me, count), [late_grads])
    expert_grads += [replica_scatter(grads.reshape(2, -1, width)) for grads in late_grads]
    d_normed_two, acts, expert_grads[0] = together(d_normed_two, acts, expert_grads[0])
    acts = jnp.concatenate(acts, 1)
    down_grads = mm("tf,td->fd", acts, wide_cot).astype(BF16).reshape(mlp_experts, -1, width)

    def own_rows(whole):
        return lax.dynamic_slice_in_dim(whole, me * rows, rows, 0)

    d_norm_two = jnp.sum(d_normed_two * middle * scale_two, 0)
    d_middle = norm_back(d_normed_two, middle, scale_two, norm_two) + cotangent.astype(F32)

    d_router_two = jnp.dot(wide_normed.astype(F32).T, d_logit_two, precision=HIGHEST)
    held = gather_start(d_middle.astype(BF16))
    for step in range(rounds):
        held = gather_step(held, step)
        if step == 0:
            held, down_grads, acts, d_router_two = together(held, down_grads, acts, d_router_two)
            partial_mix = mm("tf,fd->td", acts, down_weight.reshape(-1, width)).astype(BF16)
    mix_cut = scatter_cut(scatter_start(by_distance(partial_mix, me, count)), 0)
    mix_sent, held = together([sent for _, sent in mix_cut], held)
    mix_cut = [(kept, sent) for (kept, _), sent in zip(mix_cut, mix_sent)]
    wide_middle = in_order(gather_end(held), me, wide_normed)
    down_grads = replica_scatter(down_grads)
    d_heads, terms, out_grad = heads_back(wide_middle, out_weight, heads_out, gate_one, chips)
    mix_sent, d_heads, terms, out_grad = together(mix_sent, d_heads, terms, out_grad)
    mix_cut = [(kept, sent) for (kept, _), sent in zip(mix_cut, mix_sent)]
    out_kept, out_got = chip_sum(out_grad, 0)
    mix_pairs = scatter_send(mix_cut, 0)
    raw_terms, delta = terms.reshape(2, head_count, experts, seq)
    d_projected = attend_back(projected, segments, cos, sin, d_heads, stats, delta)
    mix_pairs, d_projected, expert_grads, out_got = arrived(
        mix_pairs, d_projected, expert_grads, out_got
    )
    mix_held = scatter_add(mix_pairs)
    mix_pairs = scatter_step(mix_held, 1) if rounds > 1 else []
    chip_rounds = chips.bit_length() - 1
    grads = [
        tn_product(normed, d_projected[k]).reshape(count, chips, 2, piece, cols) for k in range(kinds)
    ]
    kept = [lax.dynamic_index_in_dim(g, core, 2, keepdims=False) for g in grads]
    sent = jnp.stack([lax.dynamic_index_in_dim(g, 1 - core, 2, keepdims=False) for g in grads])
    sent, d_projected = together(sent, d_projected)
    got = swap(sent, "core", 1)
    d_logit_one = router_back(jnp.sum(raw_terms, 0).T, gate_one)
    share = mm("ktf,kdf->td", d_projected, weight) + by_router(d_logit_one, router_one)
    mix_pairs, share, got = arrived(mix_pairs, share.astype(BF16), got)
    pair = [add_low(one, new) for one, new in zip(kept, got)]
    out_pair = add_low(out_kept, out_got)

    def piece_of(owner):
        parts = [lax.dynamic_index_in_dim(one, owner, 1, keepdims=False) for one in pair]
        parts.append(lax.dynamic_index_in_dim(out_pair, owner, 1, keepdims=False))
        return jnp.concatenate([part.reshape(-1, cols) for part in parts], 0)

    held = scatter_start([piece_of(chip ^ r) for r in range(chips)], "chip")
    pairs = scatter_step(held, 0, "chip") if chip_rounds else []
    came = [got for _, got in pairs]
    d_normed, ((came, down_grads),) = scatter_sum(
        by_distance(share, me, count), [(came, down_grads)]
    )
    pairs = [(kept, got) for (kept, _), got in zip(pairs, came)]
    if chip_rounds:
        pairs, d_logit_one = arrived(pairs, d_logit_one)
    held = scatter_add(pairs) if chip_rounds else held
    own_scale = own_rows(scale_one)
    d_norm_one = jnp.sum(d_normed * own_hidden * own_scale, 0)
    d_router_one = jnp.dot(normed.astype(F32).T, d_logit_one, precision=HIGHEST)
    for step in range(1, chip_rounds):
        pairs = scatter_step(held, step, "chip")
        if step == 1:
            pairs, d_router_one, d_norm_one = arrived(pairs, d_router_one, d_norm_one)
        held = scatter_add(pairs)
    own = scatter_end(held).astype(BF16)
    own, out_own = jnp.split(own, [kinds * count * piece], 0)
    own = own.reshape(kinds, count, piece, cols)
    out_own = out_own.reshape(experts, count, piece, cols)
    input_grad = norm_back(d_normed, own_hidden, own_scale, norm_one) + d_middle

    parts = [lax.dynamic_index_in_dim(own, me ^ r, 1, keepdims=False) for r in range(count)]
    parts = [parts[0]] + [swap(parts[r], "shard", r) for r in range(1, count)]
    own = jnp.concatenate([pick(parts, me ^ owner) for owner in range(count)], -1)
    out_own = jnp.concatenate([out_own[:, owner] for owner in range(count)], -1)
    own = own.reshape(-1, width)
    grain = 16 * len(bit_orders(chips))
    out_own = out_own.reshape(-1, width)
    out_own = jnp.pad(out_own, ((0, -out_own.shape[0] % grain), (0, 0)))
    out_held = gather_start(out_own, "chip")
    for step in range(chip_rounds):
        out_held = gather_step(out_held, step, "chip")
    own, out_held = together(own, out_held)
    out_whole = in_order(gather_end(out_held), chip)
    out_other = swap(out_whole, "core", 1)
    out_whole, out_other = [both.reshape(chips, -1, width) for both in (out_whole, out_other)]
    (out_grad,) = lay_out(core, out_whole, out_other, experts, piece, 0)
    sums = jnp.concatenate([d_norm_one[None], d_norm_two[None], d_router_one.T, d_router_two.T], 0)
    sums = scatter_small(
        [lax.dynamic_slice_in_dim(sums, (me ^ r) * own_d, own_d, 1) for r in range(count)]
    )
    high = sums.astype(BF16)
    ride = jnp.stack([high, (sums - high.astype(F32)).astype(BF16)]).reshape(-1)
    own_rows_count = own.shape[0]
    ride_rows = -(-ride.shape[0] // width)
    ride_rows += -(own_rows_count + ride_rows) % grain
    ride = jnp.pad(ride, (0, ride_rows * width - ride.shape[0])).reshape(ride_rows, width)
    own = jnp.concatenate([own, ride], 0)
    gate_grads, up_grads = [
        jnp.stack([grads[kind] for grads in expert_grads]).astype(F32).transpose(0, 2, 1)
        for kind in range(2)
    ]
    down_grads = down_grads.astype(F32)
    own, gate_grads, up_grads, down_grads = together(own, gate_grads, up_grads, down_grads)
    held = gather_start(own, "chip")
    for step in range(chip_rounds):
        held = gather_step(held, step, "chip")
    mix_held = scatter_add(mix_pairs) if mix_pairs else mix_held
    for step in range(2, rounds):
        mix_held = scatter_add(scatter_step(mix_held, step))
    output = (middle + scatter_end(mix_held)).astype(BF16)
    held, out_grad = together(held, out_grad)
    whole = in_order(gather_end(held), chip)
    other = swap(whole, "core", 1)
    whole, other = [both.reshape(chips, -1, width) for both in (whole, other)]
    rides = jnp.concatenate([whole[:, own_rows_count:], other[:, own_rows_count:]], 0)
    rides = rides.reshape(owners, -1)[:, : 2 * sums.size].astype(F32)
    sums = jnp.sum(rides.reshape(2 * owners, -1), 0).reshape(sums.shape)
    kv_grad, query_grad = lay_out(core, whole, other, experts, piece, 2)
    return (
        output,
        input_grad,
        sums[0],
        sums[2 : 2 + experts].T,
        kv_grad,
        query_grad,
        out_grad,
        sums[1],
        sums[2 + experts :].T,
        gate_grads,
        up_grads,
        down_grads,
    )


def solution(mesh):
    devices = mesh.devices
    mesh = Mesh(devices.reshape(-1, 2, devices.shape[1]), ("chip", "core", "shard"))
    return jax.shard_map(
        on_device,
        mesh=mesh,
        in_specs=(
            P(("chip", "core", "shard"), None),
            P(("chip", "core", "shard")),
            P("shard"),
            P("shard", None),
            P("shard", None),
            P(None, "shard", None),
            P(None, "shard", None),
            P("shard"),
            P("shard", None),
            P(None, None, "shard"),
            P(None, None, "shard"),
            P(None, "shard", None),
            P(("chip", "core", "shard"), None),
        ),
        out_specs=(
            P(("chip", "core", "shard"), None),
            P(("chip", "core", "shard"), None),
            P("shard"),
            P("shard", None),
            P("shard", None),
            P(None, "shard", None),
            P(None, "shard", None),
            P("shard"),
            P("shard", None),
            P(None, None, ("shard", "chip", "core")),
            P(None, None, ("shard", "chip", "core")),
            P(None, ("shard", "chip", "core"), None),
        ),
        check_vma=False,
    )
```

```python
import jax
import jax.numpy as jnp
from jax import lax
from jax.experimental import pallas as pl
from jax.experimental.pallas import tpu as pltpu
from jax.sharding import Mesh, PartitionSpec as P

HEAD = 128
WIN = 1024
EPSILON = 1e-06
THETA = 10000.0
HIGHEST = lax.Precision.HIGHEST
BF16 = jnp.bfloat16
F32 = jnp.float32
LOG2E = 1.4426950408889634
MIB = 1 << 20
QUERY_ROWS = 256


def swap(value, axis, bits):
    count = lax.axis_size(axis)
    return lax.ppermute(value, axis, [(i, i ^ bits) for i in range(count)])


def together(*values):
    return lax.optimization_barrier(values)


def bit_orders(count):
    bits = [1 << b for b in range(count.bit_length() - 1)]
    return [bits[i:] + bits[:i] for i in range(len(bits))] or [[]]


def ways(held, axis):
    orders = bit_orders(lax.axis_size(axis))
    return [(orders[i % len(orders)], part) for i, part in enumerate(held)]


def gather_start(block, axis="shard"):
    orders = bit_orders(lax.axis_size(axis))
    return [{0: part} for part in together(*jnp.split(block, len(orders), 0))]


def gather_step(held, step, axis="shard"):
    after = []
    for order, have in ways(held, axis):
        bit = order[step]
        after.append({**have, **{r ^ bit: swap(v, axis, bit) for r, v in have.items()}})
    return after


def gather_end(held):
    return [jnp.concatenate([have[r] for have in held], 0) for r in range(len(held[0]))]


def gather_blocks(block, axis="shard"):
    held = gather_start(block, axis)
    for step in range(len(bit_orders(lax.axis_size(axis))[0])):
        held = gather_step(held, step, axis)
    return gather_end(held)


def scatter_start(blocks, axis="shard"):
    orders = bit_orders(lax.axis_size(axis))
    held = [dict() for _ in orders]
    for r, block in enumerate(blocks):
        for have, part in zip(held, jnp.split(block, len(orders), 0)):
            have[r] = part
    return held


def scatter_cut(held, step, axis="shard"):
    cut = []
    for order, have in ways(held, axis):
        bit = order[-1 - step]
        kept = {r: v for r, v in have.items() if not r & bit}
        cut.append((kept, jnp.concatenate([have[r ^ bit].astype(BF16) for r in kept], 0)))
    sent = together(*[sent for _, sent in cut])
    return [(kept, new) for (kept, _), new in zip(cut, sent)]


def scatter_send(cut, step, axis="shard"):
    pairs = []
    for order, (kept, sent) in ways(cut, axis):
        pairs.append((kept, swap(sent, axis, order[-1 - step])))
    return pairs


def arrived(pairs, *beside):
    got, *beside = together([got for _, got in pairs], *beside)
    return [(kept, new) for (kept, _), new in zip(pairs, got)], *beside


def scatter_step(held, step, axis="shard"):
    return scatter_send(scatter_cut(held, step, axis), step, axis)


def scatter_add(pairs):
    held = []
    for kept, got in pairs:
        got = jnp.split(got, len(kept), 0)
        held.append({r: kept[r].astype(F32) + new.astype(F32) for r, new in zip(kept, got)})
    return held


def scatter_end(held):
    return jnp.concatenate([have[0] for have in held], 0)


def scatter_sum(blocks, beside=(), axis="shard"):
    held = scatter_start(blocks, axis)
    beside = list(beside)
    for step in range(len(bit_orders(lax.axis_size(axis))[0])):
        pairs = scatter_step(held, step, axis)
        if step < len(beside):
            pairs, beside[step] = arrived(pairs, beside[step])
        held = scatter_add(pairs)
    return scatter_end(held), beside


def scatter_small(blocks, axis="shard"):
    total = blocks[0]
    for r in range(1, lax.axis_size(axis)):
        total = total + swap(blocks[r], axis, r)
    return total


REPLICAS = ("chip", "core")


def replica_scatter(whole):
    return lax.psum_scatter(whole, REPLICAS, scatter_dimension=1, tiled=True)


def chip_sum(whole, axis):
    core = lax.axis_index("core")
    kept = lax.dynamic_index_in_dim(whole, core, axis, keepdims=False)
    sent = lax.dynamic_index_in_dim(whole, 1 - core, axis, keepdims=False)
    return kept, swap(sent, "core", 1)


def add_low(kept, got):
    return (kept.astype(F32) + got.astype(F32)).astype(BF16)


def pick(options, index):
    chosen = options[0]
    for i, option in enumerate(options[1:], 1):
        chosen = jnp.where(index == i, option, chosen)
    return chosen


def in_order(blocks, me, base=None):
    rows = blocks[0].shape[0]
    whole = base
    if base is None:
        whole = jnp.zeros((rows * len(blocks),) + blocks[0].shape[1:], blocks[0].dtype)
    for r, block in enumerate(blocks):
        start = ((me ^ r) * rows,) + (0,) * (block.ndim - 1)
        whole = lax.dynamic_update_slice(whole, block, start)
    return whole


def by_distance(whole, me, count):
    rows = whole.shape[0] // count
    return [lax.dynamic_slice_in_dim(whole, (me ^ r) * rows, rows, 0) for r in range(count)]


def rotation_tables(length):
    half = HEAD // 2
    frequency = THETA ** (-jnp.arange(half, dtype=F32) / half)
    angle = jnp.arange(length, dtype=F32)[:, None] * frequency[None, :]
    cos, sin = jnp.cos(angle), jnp.sin(angle)
    return jnp.concatenate([cos, cos], 1), jnp.concatenate([-sin, sin], 1)


def turn(head, cos, sin):
    return head * cos + pltpu.roll(head, HEAD // 2, 1) * sin


def nt(a, b):
    return lax.dot_general(a, b, (((1,), (1,)), ((), ())), preferred_element_type=F32)


def nn(a, b):
    return lax.dot_general(a, b, (((1,), (0,)), ((), ())), preferred_element_type=F32)


def tn(a, b):
    return lax.dot_general(a, b, (((0,), (0,)), ((), ())), preferred_element_type=F32)


def project_kernel(normed, weight, cos, sin, out):
    kind = pl.program_id(1)
    product = nn(normed[...], weight[0])

    @pl.when(kind == 1)
    def _():
        out[0] = product.astype(BF16)

    @pl.when(kind != 1)
    def _():
        for start in range(0, product.shape[1], HEAD):
            head = product[:, start : start + HEAD]
            out[0, :, start : start + HEAD] = turn(head, cos[...], sin[...]).astype(BF16)


def project(normed, weight, cos, sin):
    seq, width = normed.shape
    kinds, _, cols = weight.shape
    rows = seq
    once = dict(pipeline_mode=pl.Buffered(1))
    return pl.pallas_call(
        project_kernel,
        grid=(seq // rows, kinds),
        in_specs=[
            pl.BlockSpec((rows, width), lambda i, k: (i, 0), **once),
            pl.BlockSpec((1, width, cols), lambda i, k: (k, 0, 0)),
            pl.BlockSpec((rows, HEAD), lambda i, k: (i, 0), **once),
            pl.BlockSpec((rows, HEAD), lambda i, k: (i, 0), **once),
        ],
        out_specs=pl.BlockSpec((1, rows, cols), lambda i, k: (k, i, 0)),
        out_shape=jax.ShapeDtypeStruct((kinds, seq, cols), BF16),
        compiler_params=pltpu.CompilerParams(vmem_limit_bytes=48 * MIB),
        cost_estimate=pl.CostEstimate(
            flops=2 * seq * width * kinds * cols,
            bytes_accessed=2 * (seq * width + kinds * cols * (width + seq)),
            transcendentals=0,
        ),
    )(normed, weight, cos, sin)


def key_span(block):
    low = max(0, block * QUERY_ROWS - WIN + 1) // QUERY_ROWS * QUERY_ROWS
    return low, (block + 1) * QUERY_ROWS


def forbid(query_segment, key_segment, query_place, key_place):
    distance = query_place - key_place
    allowed = (query_segment == key_segment) & (distance >= 0) & (distance < WIN)
    return jnp.where(allowed, 0.0, -1e30).astype(F32)


def attend_kernel(experts, blocks, seg_col, seg_row, keys, values, *rest):
    queries, (out, stats, bias) = rest[:experts], rest[experts:]
    block, head = pl.program_id(0), pl.program_id(1)
    factor = HEAD ** (-0.5) * LOG2E

    def step(at):
        low, high = key_span(at)
        span = high - low

        @pl.when(head == 0)
        def _():
            shape = (QUERY_ROWS, span)
            bias[:, :span] = forbid(
                seg_col[...],
                seg_row[:, low:high],
                at * QUERY_ROWS + lax.broadcasted_iota(jnp.int32, shape, 0),
                low + lax.broadcasted_iota(jnp.int32, shape, 1),
            )

        for expert in range(experts):
            scores = nt(queries[expert][0], keys[0, low:high]) + bias[:, :span]
            top = jnp.max(scores, -1, keepdims=True)
            weights = jnp.exp2((scores - top) * factor)
            total = jnp.sum(weights, -1, keepdims=True)
            mixed = nn(weights.astype(BF16), values[0, low:high]) / total
            level = jnp.broadcast_to(top * factor + jnp.log2(total), (QUERY_ROWS, HEAD)).T
            out[expert] = mixed.astype(BF16)
            stats[0, expert : expert + 1, :] = level[0:1, :]

    for at in range(blocks):
        pl.when(block == at)(lambda at=at: step(at))


def attend(projected, segments):
    kinds, seq, cols = projected.shape
    experts, heads, blocks = kinds - 2, cols // HEAD, seq // QUERY_ROWS
    widest = max(high - low for low, high in map(key_span, range(blocks)))
    pairs = sum(high - low for low, high in map(key_span, range(blocks))) * QUERY_ROWS
    query_specs = [
        pl.BlockSpec((1, QUERY_ROWS, HEAD), lambda i, h, e=e: (2 + e, i, h)) for e in range(experts)
    ]
    return pl.pallas_call(
        lambda *refs: attend_kernel(experts, blocks, *refs),
        grid=(blocks, heads),
        in_specs=[
            pl.BlockSpec((QUERY_ROWS, 1), lambda i, h: (i, 0)),
            pl.BlockSpec((1, seq), lambda i, h: (0, 0)),
            pl.BlockSpec((1, seq, HEAD), lambda i, h: (0, 0, h)),
            pl.BlockSpec((1, seq, HEAD), lambda i, h: (1, 0, h)),
        ]
        + query_specs,
        out_specs=[
            pl.BlockSpec((experts, QUERY_ROWS, HEAD), lambda i, h: (0, i, h)),
            pl.BlockSpec((1, experts, QUERY_ROWS), lambda i, h: (h, 0, i)),
        ],
        out_shape=[
            jax.ShapeDtypeStruct((experts, seq, cols), BF16),
            jax.ShapeDtypeStruct((heads, experts, seq), F32),
        ],
        scratch_shapes=[pltpu.VMEM((QUERY_ROWS, widest), F32)],
        compiler_params=pltpu.CompilerParams(vmem_limit_bytes=48 * MIB),
        cost_estimate=pl.CostEstimate(
            flops=8 * pairs * experts * heads * HEAD,
            bytes_accessed=2 * seq * cols * (2 + 2 * experts),
            transcendentals=pairs * experts * heads,
        ),
    )(segments[:, None], segments[None, :], *([projected] * (2 + experts)))


def attend_back_kernel(experts, blocks, seg_row, seg_col, cos, sin, keys, values, *rest):
    queries = rest[:experts]
    d_heads, stats, delta, out, bias, d_keys, d_values = rest[experts:]
    head, block = pl.program_id(0), pl.program_id(1)
    scale = HEAD ** (-0.5)
    factor = scale * LOG2E

    @pl.when(block == 0)
    def _():
        d_keys[...] = jnp.zeros_like(d_keys)
        d_values[...] = jnp.zeros_like(d_values)

    def step(at):
        low, high = key_span(at)
        span = high - low
        own = slice(at * QUERY_ROWS, (at + 1) * QUERY_ROWS)

        @pl.when(head == 0)
        def _():
            shape = (span, QUERY_ROWS)
            bias[at, :span, :] = forbid(
                seg_row[...],
                seg_col[low:high],
                at * QUERY_ROWS + lax.broadcasted_iota(jnp.int32, shape, 1),
                low + lax.broadcasted_iota(jnp.int32, shape, 0),
            )

        for expert in range(experts):
            query = queries[expert][0]
            d_head = d_heads[expert]
            key, value = keys[0, low:high], values[0, low:high]
            scores = nt(key, query) * factor + bias[at, :span, :]
            probs = jnp.exp2(scores - stats[0, expert : expert + 1, :])
            d_probs = nt(value, d_head)
            d_scores = (probs * (d_probs - delta[0, expert : expert + 1, :])).astype(BF16)
            d_values[low:high] += nn(probs.astype(BF16), d_head)
            d_keys[low:high] += nn(d_scores, query)
            d_query = tn(d_scores, key) * scale
            out[2 + expert, own, :] = turn(d_query, cos[own], -sin[own]).astype(BF16)

    for at in range(blocks):
        pl.when(block == at)(lambda at=at: step(at))

    @pl.when(block == blocks - 1)
    def _():
        out[0] = turn(d_keys[...] * scale, cos[...], -sin[...]).astype(BF16)
        out[1] = d_values[...].astype(BF16)


def attend_back(projected, segments, cos, sin, d_heads, stats, delta):
    kinds, seq, cols = projected.shape
    experts, heads, blocks = kinds - 2, cols // HEAD, seq // QUERY_ROWS
    widest = max(high - low for low, high in map(key_span, range(blocks)))
    pairs = sum(high - low for low, high in map(key_span, range(blocks))) * QUERY_ROWS
    query_specs = [
        pl.BlockSpec((1, QUERY_ROWS, HEAD), lambda h, i, e=e: (2 + e, i, h)) for e in range(experts)
    ]
    row_spec = pl.BlockSpec((1, experts, QUERY_ROWS), lambda h, i: (h, 0, i))
    return pl.pallas_call(
        lambda *refs: attend_back_kernel(experts, blocks, *refs),
        grid=(heads, blocks),
        in_specs=[
            pl.BlockSpec((1, QUERY_ROWS), lambda h, i: (0, i)),
            pl.BlockSpec((seq, 1), lambda h, i: (0, 0)),
            pl.BlockSpec((seq, HEAD), lambda h, i: (0, 0)),
            pl.BlockSpec((seq, HEAD), lambda h, i: (0, 0)),
            pl.BlockSpec((1, seq, HEAD), lambda h, i: (0, 0, h)),
            pl.BlockSpec((1, seq, HEAD), lambda h, i: (1, 0, h)),
        ]
        + query_specs
        + [
            pl.BlockSpec((experts, QUERY_ROWS, HEAD), lambda h, i: (0, i, h)),
            row_spec,
            row_spec,
        ],
        out_specs=pl.BlockSpec((kinds, seq, HEAD), lambda h, i: (0, 0, h)),
        out_shape=jax.ShapeDtypeStruct((kinds, seq, cols), BF16),
        scratch_shapes=[
            pltpu.VMEM((blocks, widest, QUERY_ROWS), F32),
            pltpu.VMEM((seq, HEAD), F32),
            pltpu.VMEM((seq, HEAD), F32),
        ],
        compiler_params=pltpu.CompilerParams(vmem_limit_bytes=48 * MIB),
        cost_estimate=pl.CostEstimate(
            flops=20 * pairs * experts * heads * HEAD,
            bytes_accessed=2 * seq * cols * (2 * kinds + experts),
            transcendentals=pairs * experts * heads,
        ),
    )(
        segments[None, :],
        segments[:, None],
        cos,
        sin,
        *([projected] * (2 + experts)),
        d_heads,
        stats,
        delta,
    )


def norm_back(d_normed, hidden, inv_scale, gain):
    scaled_grad = d_normed * gain
    return inv_scale * scaled_grad - hidden * inv_scale**3 * jnp.mean(
        scaled_grad * hidden, -1, keepdims=True
    )


def swiglu_kernel(expert, gate_pre, up_pre, d_act, gates, d_both, act, term):
    rows, width = gate_pre.shape
    lanes, step = 128, 32
    lanes = lanes if width % lanes == 0 else width
    step = step if rows % step == 0 else rows

    def part(i, carry):
        at = pl.ds(pl.multiple_of(i * step, step), step)
        gate = gates[at, expert : expert + 1]
        total = jnp.zeros((step, lanes), F32)
        for start in range(0, width, lanes):
            cut = slice(start, start + lanes)
            pre = gate_pre[at, cut].astype(F32)
            up = up_pre[at, cut].astype(F32)
            raw = d_act[at, cut].astype(F32)
            sigmoid = 0.5 * jnp.tanh(0.5 * pre) + 0.5
            silu = pre * sigmoid
            inner = silu * up
            total = total + inner * raw
            act[at, cut] = (inner * gate).astype(BF16)
            d_inner = raw * gate
            slope = sigmoid + silu * (1.0 - sigmoid)
            d_both[at, cut] = (d_inner * up * slope).astype(BF16)
            d_both[at, width + start : width + start + lanes] = (d_inner * silu).astype(BF16)
        term[at, :] = jnp.sum(total, -1, keepdims=True)
        return carry

    lax.fori_loop(0, rows // step, part, 0)


def swiglu(expert, gate_pre, up_pre, d_act, gates):
    seq, hidden = gate_pre.shape
    rows = 256 if seq % 256 == 0 else seq
    return pl.pallas_call(
        lambda *refs: swiglu_kernel(expert, *refs),
        grid=(seq // rows,),
        in_specs=[
            pl.BlockSpec((rows, hidden), lambda i: (i, 0)),
            pl.BlockSpec((rows, hidden), lambda i: (i, 0)),
            pl.BlockSpec((rows, hidden), lambda i: (i, 0)),
            pl.BlockSpec((rows, gates.shape[1]), lambda i: (i, 0)),
        ],
        out_specs=[
            pl.BlockSpec((rows, 2 * hidden), lambda i: (i, 0)),
            pl.BlockSpec((rows, hidden), lambda i: (i, 0)),
            pl.BlockSpec((rows, 1), lambda i: (i, 0)),
        ],
        out_shape=[
            jax.ShapeDtypeStruct((seq, 2 * hidden), BF16),
            jax.ShapeDtypeStruct((seq, hidden), BF16),
            jax.ShapeDtypeStruct((seq, 1), F32),
        ],
        compiler_params=pltpu.CompilerParams(vmem_limit_bytes=48 * MIB),
        cost_estimate=pl.CostEstimate(
            flops=20 * seq * hidden, bytes_accessed=12 * seq * hidden, transcendentals=seq * hidden
        ),
    )(gate_pre, up_pre, d_act, gates)


def heads_back_kernel(d_middle, out_weight, heads_out, gates, d_heads, terms, grads, total):
    block = pl.program_id(0)
    experts, cols, _ = out_weight.shape
    rows = d_middle.shape[0]

    @pl.when(block == 0)
    def _():
        total[...] = jnp.zeros_like(total)

    lane = lax.broadcasted_iota(jnp.int32, (rows, HEAD), 1)
    table = jnp.zeros((rows, HEAD), F32)
    count = experts * (cols // HEAD)
    for expert in range(experts):
        gate = gates[:, expert : expert + 1]
        back = nt(d_middle[...], out_weight[expert])
        heads = heads_out[expert].astype(F32)
        pairing = back * heads
        for head in range(cols // HEAD):
            term = jnp.sum(pairing[:, head * HEAD : (head + 1) * HEAD], -1, keepdims=True)
            at = head * experts + expert
            table = table + jnp.where(lane == at, term, 0.0)
            table = table + jnp.where(lane == count + at, term * gate, 0.0)
        d_heads[expert] = (back * gate).astype(BF16)
        total[expert] += tn((heads * gate).astype(BF16), d_middle[...])
    terms[...] = table.T[: 2 * count]

    @pl.when(block == pl.num_programs(0) - 1)
    def _():
        _, _, chips, blocks, piece, width = grads.shape
        for chip in range(chips):
            for core in range(2):
                at = (2 * chip + core) * piece
                for j in range(blocks):
                    cut = slice(j * width, (j + 1) * width)
                    grads[core, :, chip, j] = total[:, at : at + piece, cut].astype(BF16)


def heads_back(d_middle, out_weight, heads_out, gates, chips):
    experts, seq, cols = heads_out.shape
    depth = d_middle.shape[1]
    rows = 512 if seq % 512 == 0 else seq
    count = experts * (cols // HEAD)
    split = (2, experts, chips, depth // cols, cols // chips // 2, cols)
    return pl.pallas_call(
        heads_back_kernel,
        grid=(seq // rows,),
        in_specs=[
            pl.BlockSpec((rows, depth), lambda i: (i, 0)),
            pl.BlockSpec((experts, cols, depth), lambda i: (0, 0, 0)),
            pl.BlockSpec((experts, rows, cols), lambda i: (0, i, 0)),
            pl.BlockSpec((rows, experts), lambda i: (i, 0)),
        ],
        out_specs=[
            pl.BlockSpec((experts, rows, cols), lambda i: (0, i, 0)),
            pl.BlockSpec((2 * count, rows), lambda i: (0, i)),
            pl.BlockSpec(split, lambda i: (0,) * 6),
        ],
        out_shape=[
            jax.ShapeDtypeStruct((experts, seq, cols), BF16),
            jax.ShapeDtypeStruct((2 * count, seq), F32),
            jax.ShapeDtypeStruct(split, BF16),
        ],
        scratch_shapes=[pltpu.VMEM((experts, cols, depth), F32)],
        compiler_params=pltpu.CompilerParams(vmem_limit_bytes=56 * MIB),
        cost_estimate=pl.CostEstimate(
            flops=8 * seq * depth * cols * experts // 2,
            bytes_accessed=2 * (seq * depth + 2 * experts * cols * (seq + depth)),
            transcendentals=0,
        ),
    )(d_middle, out_weight, heads_out, gates)


def lay_out_kernel(beside, core, mine, other, *outs):
    experts, piece, width = outs[-1].shape

    def lay(source):
        for kind in range(beside):
            rows_of = source[0, kind * piece : (kind + 1) * piece]
            outs[0][:, kind * width : (kind + 1) * width] = rows_of.astype(F32)
        for expert in range(experts):
            at = (beside + expert) * piece
            outs[-1][expert] = source[0, at : at + piece].astype(F32)

    pl.when(core[0] == pl.program_id(1))(lambda: lay(mine))
    pl.when(core[0] != pl.program_id(1))(lambda: lay(other))


def lay_out(core, mine, other, experts, piece, beside):
    chips, rows, width = mine.shape
    own = 2 * chips * piece
    out_specs = [pl.BlockSpec((experts, piece, width), lambda j, k: (0, 2 * j + k, 0))]
    out_shape = [jax.ShapeDtypeStruct((experts, own, width), F32)]
    if beside:
        out_specs.insert(0, pl.BlockSpec((piece, beside * width), lambda j, k: (2 * j + k, 0)))
        out_shape.insert(0, jax.ShapeDtypeStruct((own, beside * width), F32))
    return pl.pallas_call(
        lambda *refs: lay_out_kernel(beside, *refs),
        grid=(chips, 2),
        in_specs=[
            pl.BlockSpec(memory_space=pltpu.SMEM),
            pl.BlockSpec((1, rows, width), lambda j, k: (j, 0, 0)),
            pl.BlockSpec((1, rows, width), lambda j, k: (j, 0, 0)),
        ],
        out_specs=out_specs,
        out_shape=out_shape,
        compiler_params=pltpu.CompilerParams(vmem_limit_bytes=48 * MIB),
        cost_estimate=pl.CostEstimate(
            flops=0,
            bytes_accessed=4 * chips * rows * width + 4 * own * width * (beside + experts),
            transcendentals=0,
        ),
    )(core.reshape(1).astype(jnp.int32), mine, other)


def router_back(d_gates, gates):
    return gates * (d_gates - jnp.sum(gates * d_gates, -1, keepdims=True))


def tn_product(a, b):
    return mm("td,tf->df", a, b).astype(BF16)


def by_router(d_logit, router):
    columns = [(d_logit[:, e : e + 1], router[:, e].astype(F32)) for e in range(router.shape[1])]
    return sum(d * row[None, :] for d, row in columns)


def mm(spec, a, b):
    return jnp.einsum(spec, a, b, preferred_element_type=F32)


def on_device(
    hidden_in,
    segment_ids,
    attn_norm,
    attn_router,
    kv_weight,
    query_weight,
    out_weight,
    mlp_norm,
    mlp_router,
    gate_weight,
    up_weight,
    down_weight,
    cotangent,
):
    rows, width = hidden_in.shape
    count = lax.axis_size("shard")
    me = lax.axis_index("shard")
    core = lax.axis_index("core")
    seq = rows * count
    own_d = kv_weight.shape[0]
    experts = query_weight.shape[0]
    cols = query_weight.shape[2] // count
    head_count = cols // HEAD
    mlp_experts = gate_weight.shape[0]
    score_scale = HEAD ** (-0.5)

    cos, sin = rotation_tables(seq)

    small = jnp.concatenate(
        [
            attn_norm,
            mlp_norm,
            attn_router.T.reshape(-1),
            mlp_router.T.reshape(-1),
            segment_ids.astype(BF16),
        ]
    )
    small = jnp.pad(small, (0, -small.shape[0] % (16 * cols))).reshape(-1, cols)
    small_rows = small.shape[0]
    kinds = 2 + experts
    chips, chip = lax.axis_size("chip"), lax.axis_index("chip")
    owners = 2 * chips
    replica = 2 * chip + core
    piece = own_d // owners

    def columns(owner, start, size):
        at = owner * cols
        return jnp.stack(
            [lax.dynamic_slice(kv_weight, (start, at), (size, cols))]
            + [lax.dynamic_slice(kv_weight, (start, count * cols + at), (size, cols))]
            + [lax.dynamic_slice(w, (start, at), (size, cols)) for w in query_weight]
        )

    def message(owner):
        return jnp.concatenate([columns(owner, replica * piece, piece).reshape(-1, cols), small], 0)

    fetched = [swap(message(me ^ r), "shard", r) for r in range(1, count)]
    held = gather_step(gather_start(hidden_in), 0)
    joined = [jnp.concatenate([gate_weight[0], up_weight[0]], 1)]
    fetched, held, joined = together(fetched, held, joined)
    small = [small] + [rows_of[-small_rows:] for rows_of in fetched]
    fetched = jnp.stack([rows_of[:-small_rows].reshape(kinds, piece, cols) for rows_of in fetched])
    shares = lax.all_gather(fetched, REPLICAS, axis=0)
    weight = jnp.zeros((kinds, width, cols), BF16)
    weight = lax.dynamic_update_slice(weight, columns(me, 0, own_d), (0, me * own_d, 0))
    rounds = len(bit_orders(count)[0])
    for step in range(1, rounds):
        held = gather_step(held, step)
    held, weight = together(held, weight)
    small = jnp.stack([pick(small, me ^ owner) for owner in range(count)]).reshape(count, -1)
    bounds = [0]
    for size in (own_d, own_d, own_d * experts, own_d * mlp_experts, rows):
        bounds.append(bounds[-1] + size)
    pieces = [small[:, a:b] for a, b in zip(bounds, bounds[1:])]
    norm_one = pieces[0].reshape(width).astype(F32)
    norm_two = pieces[1].reshape(width).astype(F32)
    router_one = pieces[2].reshape(count, experts, own_d).transpose(0, 2, 1).reshape(width, experts)
    router_two = (
        pieces[3].reshape(count, mlp_experts, own_d).transpose(0, 2, 1).reshape(width, mlp_experts)
    )
    segments = pieces[4].reshape(seq).astype(jnp.int32)

    hidden_low = in_order(gather_end(held), me)
    hidden = hidden_low.astype(F32)
    scale_one = lax.rsqrt(jnp.mean(hidden * hidden, -1, keepdims=True) + EPSILON)
    normed = (hidden * scale_one * norm_one).astype(BF16)
    normed, cos, sin, weight, shares = together(normed, cos, sin, weight, shares)
    for r in range(1, count):
        rows_of = shares[:, r - 1].transpose(1, 0, 2, 3).reshape(kinds, own_d, cols)
        weight = lax.dynamic_update_slice(weight, rows_of, (0, (me ^ r) * own_d, 0))
    gate_one = jax.nn.softmax(jnp.dot(normed, router_one, preferred_element_type=F32), -1)
    projected = project(normed, weight, cos, sin)

    cot_ready, _ = together(cotangent, weight)
    wide_cot = lax.all_gather(cot_ready, "shard", axis=0, tiled=True)
    heads_out, stats = attend(projected, segments)
    heads_out, wide_cot = together(heads_out, wide_cot)
    for expert in range(experts):
        weighted = gate_one[:, expert : expert + 1] * jnp.dot(
            heads_out[expert], out_weight[expert], preferred_element_type=F32
        )
        attn_mix = weighted if expert == 0 else attn_mix + weighted
    own_hidden = hidden_in.astype(F32)
    attn_mix, wide_cot = together(attn_mix.astype(BF16), wide_cot)
    d_act = [mm("td,fd->tf", wide_cot, down_weight[0]).astype(BF16)]
    joined += [jnp.concatenate(both, 1) for both in zip(gate_weight[1:], up_weight[1:])]
    attn_sum, ((wide_cot, d_act), joined) = scatter_sum(
        by_distance(attn_mix, me, count), [(wide_cot, d_act), joined]
    )
    middle = own_hidden + attn_sum
    scale_two = lax.rsqrt(jnp.mean(middle * middle, -1, keepdims=True) + EPSILON)
    normed_two = (middle * scale_two * norm_two).astype(BF16)

    for expert in range(1, mlp_experts):
        d_act.append(mm("td,fd->tf", wide_cot, down_weight[expert]).astype(BF16))
    held = gather_start(normed_two)
    for step in range(rounds):
        held = gather_step(held, step)
    held, d_act = together(held, d_act)
    wide_normed = in_order(gather_end(held), me, hidden_low)
    wide_gate = jax.nn.softmax(jnp.dot(wide_normed, router_two, preferred_element_type=F32), -1)
    d_both = []
    acts = []
    gate_terms = []
    expert_grads = []
    for expert in range(mlp_experts):
        gate_pre = mm("td,df->tf", wide_normed, gate_weight[expert]).astype(BF16)
        up_pre = mm("td,df->tf", wide_normed, up_weight[expert]).astype(BF16)
        both, act, term = swiglu(expert, gate_pre, up_pre, d_act[expert], wide_gate)
        if expert == 0:
            grads = mm("tf,td->fd", both, wide_normed).astype(BF16)
            grads, wide_normed = together(grads, wide_normed)
            expert_grads.append(replica_scatter(grads.reshape(2, -1, width)))
        d_both.append(both)
        acts.append(act)
        gate_terms.append(term)
    d_logit_two = router_back(jnp.concatenate(gate_terms, -1), wide_gate)
    wide_grad = sum(mm("tf,df->td", d, w) for d, w in zip(d_both, joined))
    wide_grad = (wide_grad + by_router(d_logit_two, router_two)).astype(BF16)
    wide_grad, d_both = together(wide_grad, d_both)
    late_grads = [mm("tf,td->fd", d, wide_normed).astype(BF16) for d in d_both[1:]]
    d_normed_two, (late_grads,) = scatter_sum(by_distance(wide_grad, me, count), [late_grads])
    expert_grads += [replica_scatter(grads.reshape(2, -1, width)) for grads in late_grads]
    d_normed_two, acts, expert_grads[0] = together(d_normed_two, acts, expert_grads[0])
    acts = jnp.concatenate(acts, 1)
    down_grads = mm("tf,td->fd", acts, wide_cot).astype(BF16).reshape(mlp_experts, -1, width)

    def own_rows(whole):
        return lax.dynamic_slice_in_dim(whole, me * rows, rows, 0)

    d_norm_two = jnp.sum(d_normed_two * middle * scale_two, 0)
    d_middle = norm_back(d_normed_two, middle, scale_two, norm_two) + cotangent.astype(F32)

    d_router_two = jnp.dot(wide_normed.astype(F32).T, d_logit_two, precision=HIGHEST)
    held = gather_start(d_middle.astype(BF16))
    for step in range(rounds):
        held = gather_step(held, step)
        if step == 0:
            held, down_grads, acts, d_router_two = together(held, down_grads, acts, d_router_two)
            partial_mix = mm("tf,fd->td", acts, down_weight.reshape(-1, width)).astype(BF16)
    mix_cut = scatter_cut(scatter_start(by_distance(partial_mix, me, count)), 0)
    mix_sent, held = together([sent for _, sent in mix_cut], held)
    mix_cut = [(kept, sent) for (kept, _), sent in zip(mix_cut, mix_sent)]
    wide_middle = in_order(gather_end(held), me, wide_normed)
    down_grads = replica_scatter(down_grads)
    d_heads, terms, out_grad = heads_back(wide_middle, out_weight, heads_out, gate_one, chips)
    mix_sent, d_heads, terms, out_grad = together(mix_sent, d_heads, terms, out_grad)
    mix_cut = [(kept, sent) for (kept, _), sent in zip(mix_cut, mix_sent)]
    out_kept, out_got = chip_sum(out_grad, 0)
    mix_pairs = scatter_send(mix_cut, 0)
    raw_terms, delta = terms.reshape(2, head_count, experts, seq)
    d_projected = attend_back(projected, segments, cos, sin, d_heads, stats, delta)
    mix_pairs, d_projected, expert_grads, out_got = arrived(
        mix_pairs, d_projected, expert_grads, out_got
    )
    mix_held = scatter_add(mix_pairs)
    mix_pairs = scatter_step(mix_held, 1) if rounds > 1 else []
    chip_rounds = chips.bit_length() - 1
    grads = [
        tn_product(normed, d_projected[k]).reshape(count, chips, 2, piece, cols) for k in range(kinds)
    ]
    kept = [lax.dynamic_index_in_dim(g, core, 2, keepdims=False) for g in grads]
    sent = jnp.stack([lax.dynamic_index_in_dim(g, 1 - core, 2, keepdims=False) for g in grads])
    sent, d_projected = together(sent, d_projected)
    got = swap(sent, "core", 1)
    d_logit_one = router_back(jnp.sum(raw_terms, 0).T, gate_one)
    share = mm("ktf,kdf->td", d_projected, weight) + by_router(d_logit_one, router_one)
    mix_pairs, share, got = arrived(mix_pairs, share.astype(BF16), got)
    pair = [add_low(one, new) for one, new in zip(kept, got)]
    out_pair = add_low(out_kept, out_got)

    def piece_of(owner):
        parts = [lax.dynamic_index_in_dim(one, owner, 1, keepdims=False) for one in pair]
        parts.append(lax.dynamic_index_in_dim(out_pair, owner, 1, keepdims=False))
        return jnp.concatenate([part.reshape(-1, cols) for part in parts], 0)

    held = scatter_start([piece_of(chip ^ r) for r in range(chips)], "chip")
    pairs = scatter_step(held, 0, "chip") if chip_rounds else []
    came = [got for _, got in pairs]
    d_normed, ((came, down_grads),) = scatter_sum(
        by_distance(share, me, count), [(came, down_grads)]
    )
    pairs = [(kept, got) for (kept, _), got in zip(pairs, came)]
    if chip_rounds:
        pairs, d_logit_one = arrived(pairs, d_logit_one)
    held = scatter_add(pairs) if chip_rounds else held
    own_scale = own_rows(scale_one)
    d_norm_one = jnp.sum(d_normed * own_hidden * own_scale, 0)
    d_router_one = jnp.dot(normed.astype(F32).T, d_logit_one, precision=HIGHEST)
    for step in range(1, chip_rounds):
        pairs = scatter_step(held, step, "chip")
        if step == 1:
            pairs, d_router_one, d_norm_one = arrived(pairs, d_router_one, d_norm_one)
        held = scatter_add(pairs)
    own = scatter_end(held).astype(BF16)
    own, out_own = jnp.split(own, [kinds * count * piece], 0)
    own = own.reshape(kinds, count, piece, cols)
    out_own = out_own.reshape(experts, count, piece, cols)
    input_grad = norm_back(d_normed, own_hidden, own_scale, norm_one) + d_middle

    parts = [lax.dynamic_index_in_dim(own, me ^ r, 1, keepdims=False) for r in range(count)]
    parts = [parts[0]] + [swap(parts[r], "shard", r) for r in range(1, count)]
    own = jnp.concatenate([pick(parts, me ^ owner) for owner in range(count)], -1)
    out_own = jnp.concatenate([out_own[:, owner] for owner in range(count)], -1)
    own = own.reshape(-1, width)
    grain = 16 * len(bit_orders(chips))
    out_own = out_own.reshape(-1, width)
    out_own = jnp.pad(out_own, ((0, -out_own.shape[0] % grain), (0, 0)))
    out_held = gather_start(out_own, "chip")
    for step in range(chip_rounds):
        out_held = gather_step(out_held, step, "chip")
    own, out_held = together(own, out_held)
    out_whole = in_order(gather_end(out_held), chip)
    out_other = swap(out_whole, "core", 1)
    out_whole, out_other = [both.reshape(chips, -1, width) for both in (out_whole, out_other)]
    (out_grad,) = lay_out(core, out_whole, out_other, experts, piece, 0)
    sums = jnp.concatenate([d_norm_one[None], d_norm_two[None], d_router_one.T, d_router_two.T], 0)
    sums = scatter_small(
        [lax.dynamic_slice_in_dim(sums, (me ^ r) * own_d, own_d, 1) for r in range(count)]
    )
    high = sums.astype(BF16)
    ride = jnp.stack([high, (sums - high.astype(F32)).astype(BF16)]).reshape(-1)
    own_rows_count = own.shape[0]
    ride_rows = -(-ride.shape[0] // width)
    ride_rows += -(own_rows_count + ride_rows) % grain
    ride = jnp.pad(ride, (0, ride_rows * width - ride.shape[0])).reshape(ride_rows, width)
    own = jnp.concatenate([own, ride], 0)
    gate_grads, up_grads = [
        jnp.stack([grads[kind] for grads in expert_grads]).astype(F32).transpose(0, 2, 1)
        for kind in range(2)
    ]
    down_grads = down_grads.astype(F32)
    own, gate_grads, up_grads, down_grads = together(own, gate_grads, up_grads, down_grads)
    held = gather_start(own, "chip")
    for step in range(chip_rounds):
        held = gather_step(held, step, "chip")
    mix_held = scatter_add(mix_pairs) if mix_pairs else mix_held
    for step in range(2, rounds):
        mix_held = scatter_add(scatter_step(mix_held, step))
    output = (middle + scatter_end(mix_held)).astype(BF16)
    held, out_grad = together(held, out_grad)
    whole = in_order(gather_end(held), chip)
    other = swap(whole, "core", 1)
    whole, other = [both.reshape(chips, -1, width) for both in (whole, other)]
    rides = jnp.concatenate([whole[:, own_rows_count:], other[:, own_rows_count:]], 0)
    rides = rides.reshape(owners, -1)[:, : 2 * sums.size].astype(F32)
    sums = jnp.sum(rides.reshape(2 * owners, -1), 0).reshape(sums.shape)
    kv_grad, query_grad = lay_out(core, whole, other, experts, piece, 2)
    return (
        output,
        input_grad,
        sums[0],
        sums[2 : 2 + experts].T,
        kv_grad,
        query_grad,
        out_grad,
        sums[1],
        sums[2 + experts :].T,
        gate_grads,
        up_grads,
        down_grads,
    )


def solution(mesh):
    devices = mesh.devices
    mesh = Mesh(devices.reshape(-1, 2, devices.shape[1]), ("chip", "core", "shard"))
    return jax.shard_map(
        on_device,
        mesh=mesh,
        in_specs=(
            P(("chip", "core", "shard"), None),
            P(("chip", "core", "shard")),
            P("shard"),
            P("shard", None),
            P("shard", None),
            P(None, "shard", None),
            P(None, "shard", None),
            P("shard"),
            P("shard", None),
            P(None, None, "shard"),
            P(None, None, "shard"),
            P(None, "shard", None),
            P(("chip", "core", "shard"), None),
        ),
        out_specs=(
            P(("chip", "core", "shard"), None),
            P(("chip", "core", "shard"), None),
            P("shard"),
            P("shard", None),
            P("shard", None),
            P(None, "shard", None),
            P(None, "shard", None),
            P("shard"),
            P("shard", None),
            P(None, None, ("shard", "chip", "core")),
            P(None, None, ("shard", "chip", "core")),
            P(None, ("shard", "chip", "core"), None),
        ),
        check_vma=False,
    )
```
